32 devices in a mesh: dom: 32 (over z, y, x, core).
Axes of the slice: x: 2, y: 2, z: 4, core: 2. Of those that a mesh axis runs over, the one named last changes fastest.
Arguments:
- embeddings: float32 [16384, 256], P('dom'), may hold values from -1.75 to 1.75
- emb_state: float32 [16384], P('dom'), may hold values from 0.001 to 0.1
- relations: float32 [64, 256], replicated, may hold values from -6 to 6
- rel_state: float32 [64, 256], replicated, may hold values from 0.001 to 0.1
- matching: int32 [2], replicated, may hold values from 1 to 31
- src_index: int32 [2, 8192], P(None, 'dom'), may hold values from 0 to 511
- dst_index: int32 [2, 8192], P(None, 'dom'), may hold values from 0 to 511
- rel_index: int32 [2, 8192], P(None, 'dom'), may hold values from 0 to 63
- neg_index: int32 [2, 32768], P(None, 'dom'), may hold values from 0 to 511
- counts: int32 [2, 32], P(None, 'dom'), may hold values from 1 to 256, 4096 in all within a row
Outputs:
- new_embeddings: float32 [16384, 256], P('dom')
- new_emb_state: float32 [16384], P('dom')
- new_relations: float32 [64, 256], replicated
- new_rel_state: float32 [64, 256], replicated
The draws below stay inside these ranges and needn't reach their ends.
Inputs may be any that keep to these rules, and one draw needn't show every extreme that they name: Round k pairs partition p with partition p XOR matching[k]. `counts`: some bucket of each round is full.
All inputs are finite; a program needn't handle non-finite values. No bound on the sum of `counts` on one device may be relied on, other than what follows from the above.
Results may differ from the reference program's by a relative error of at most 0.0029.
Values may be sent and summed in bfloat16 or wider, within the bound.
A program may use at most 64 MiB of HBM per device.

```python
import math
import jax
import jax.numpy as jnp
import numpy as np
from jax import lax

EMB = 256
ROWS = 512
GROUP = 256
GROUPS = 1
NEG = 1024
R = 64
ROUNDS = 2
CAP = 256
ENTITIES = 16384
ALL_EDGES = 8192
ALL_NEG = 32768
N_DOM = 32


def place_ends(values, own_key, low, largest):
    place = [jax.random.randint(jax.random.fold_in(own_key, axis), (), 0, length) for axis, length in enumerate(values.shape)]
    longest = values.shape.index(max(values.shape))
    neighbour = place[:longest] + [(place[longest] + 1) % values.shape[longest]] + place[longest + 1:]
    return values.at[tuple(place)].set(low).at[tuple(neighbour)].set(largest)


def block_scale(stream_key, extent, cuts, low, high):
    gain, own = 1.0, jax.random.fold_in(stream_key, 6)
    for axis_at, blocks in cuts:
        draws = jnp.exp(jax.random.uniform(jax.random.fold_in(own, axis_at), (blocks,), jnp.float32, low / len(cuts), high / len(cuts)))
        gain = gain * jnp.repeat(draws, extent[axis_at] // blocks).reshape([-1 if axis == axis_at else 1 for axis in range(len(extent))])
    return gain


def rank_table(amount, slope):
    loads = [(1 << 20) // math.isqrt(standing ** slope) + 1 for standing in range(1, amount + 1)]
    deviation = 1 + sum(loads) // (1 << 30)
    return np.cumsum(np.array([max(1, weight // deviation) for weight in loads]))


def skewed_ids(key, shape, amount, slope):
    table = rank_table(amount, slope)
    ticket = jax.random.randint(jax.random.fold_in(key, 1), shape, 0, int(table[amount - 1]))
    rank = jnp.searchsorted(jnp.asarray(table, jnp.int32), ticket, side="right")
    return jax.random.permutation(jax.random.fold_in(key, 2), amount)[rank].astype(jnp.int32)


def length_profile(amount, total, reach, skew):
    weights = [(1 << 20) // math.isqrt(grade ** skew) + 1 for grade in range(2, amount + 1)]
    surplus, given = total - reach - (amount - 1), [1] * (amount - 1)
    while surplus > 0:
        free = [i for i in range(amount - 1) if given[i] < reach]
        mass, remaining = sum([weights[i] for i in free]), surplus
        for i in free:
            more = min(reach - given[i], max(1, remaining * weights[i] // mass), surplus)
            given[i] = given[i] + more
            surplus = surplus - more
    return np.array([reach] + given)


def uneven(key, number_of, total, most, slope):
    if number_of == 2:
        one = jax.random.randint(key, (), max(1, total - most), min(most, total - 1) + 1)
        return jnp.stack([one, total - one])
    lengths = jnp.asarray(length_profile(number_of, total, most, slope), jnp.int32)
    twos = (number_of - 1) // 2
    giver, sink = lengths[1:1 + 2 * twos:2], lengths[2:2 + 2 * twos:2]
    slack = jnp.minimum(giver - 1, most - sink)
    passed = jax.random.randint(jax.random.fold_in(key, 1), (twos,), 0, 1 << 20) % (slack + 1)
    lengths = lengths.at[1:1 + 2 * twos:2].set(giver - passed).at[2:2 + 2 * twos:2].set(sink + passed)
    return lengths[jax.random.permutation(jax.random.fold_in(key, 2), number_of)]


def bell_draw(stream_key, shape, scale, limit, cuts=(), held_as=jnp.bfloat16):
    entries = jax.random.normal(stream_key, shape, jnp.float32) * scale
    if len(cuts) > 0:
        entries = block_scale(stream_key, shape, cuts, -0.22, 0.18) * entries
    return jnp.clip(entries, min=-limit, max=limit).astype(held_as)


def setup_inputs(seed: int = 0) -> dict:
    keys = jax.random.split(jax.random.key(seed), 11)
    return {
        "embeddings": bell_draw(keys[0], (ENTITIES, EMB), 0.3, 1.75, ((0, 32),), jnp.float32),
        "emb_state": jnp.clip(jnp.exp(math.log(0.1) - 4.6051702 * jax.random.uniform(keys[1], (ENTITIES,), jnp.float32) ** block_scale(keys[1], (ENTITIES,), ((0, 32),), -0.2, 0.2)), 0.001, 0.1),
        "relations": bell_draw(keys[2], (R, EMB), 1.0, 6.0, (), jnp.float32),
        "rel_state": jnp.clip(jnp.exp(jax.random.uniform(keys[3], (R, EMB), jnp.float32, math.log(0.001), math.log(0.1))), 0.001, 0.1),
        "matching": jax.random.randint(keys[4], (ROUNDS,), 1, N_DOM).astype(jnp.int32),
        "src_index": place_ends(skewed_ids(keys[5], (ROUNDS, ALL_EDGES), ROWS, 1), jax.random.fold_in(keys[5], 3), 0, ROWS - 1).astype(jnp.int32),
        "dst_index": place_ends(skewed_ids(keys[6], (ROUNDS, ALL_EDGES), ROWS, 2), jax.random.fold_in(keys[6], 3), 0, ROWS - 1).astype(jnp.int32),
        "rel_index": place_ends(skewed_ids(keys[7], (ROUNDS, ALL_EDGES), R, 2), jax.random.fold_in(keys[7], 3), 0, R - 1).astype(jnp.int32),
        "neg_index": place_ends(jax.random.randint(keys[8], (ROUNDS, ALL_NEG), 0, ROWS), jax.random.fold_in(keys[8], 1), 0, ROWS - 1).astype(jnp.int32),
        "counts": jax.vmap(lambda own: uneven(own, N_DOM, N_DOM * CAP // 2, CAP, 2))(jax.random.split(keys[9], ROUNDS)).reshape((ROUNDS, N_DOM)).astype(jnp.int32),
    }


LEARN_RATE = 0.1
EPSILON = 1e-06

def complex_times(values, factor):
    half_width = values.shape[-1] // 2
    val_real, val_imag = (values[..., :half_width], values[..., half_width:])
    fac_real, fac_imag = (factor[..., :half_width], factor[..., half_width:])
    return jnp.concatenate([val_real * fac_real - val_imag * fac_imag, val_real * fac_imag + val_imag * fac_real], axis=-1)

def conj_times(values, factor):
    half_width = values.shape[-1] // 2
    val_real, val_imag = (values[..., :half_width], values[..., half_width:])
    fac_real, fac_imag = (factor[..., :half_width], factor[..., half_width:])
    return jnp.concatenate([val_real * fac_real + val_imag * fac_imag, -val_real * fac_imag + val_imag * fac_real], axis=-1)

def group_terms(src_bf, dst_bf, neg_bf, rel_rows, live_edge):
    source = src_bf.astype(jnp.float32)
    target = dst_bf.astype(jnp.float32)
    query = complex_times(source, rel_rows)
    positive = lax.optimization_barrier(jnp.sum(query * target, axis=-1))
    query_bf = query.astype(jnp.bfloat16)
    scores = lax.dot_general(query_bf, neg_bf, (((1,), (1,)), ((), ())), preferred_element_type=jnp.float32)
    grad_pos = -jax.nn.sigmoid(-positive) * live_edge
    grad_score = (jax.nn.sigmoid(scores) * (live_edge / neg_bf.shape[0])[:, None]).astype(jnp.bfloat16)
    grad_query = grad_pos[:, None] * target + jnp.dot(grad_score, neg_bf, preferred_element_type=jnp.float32)
    grad_dst = grad_pos[:, None] * query
    grad_neg = lax.dot_general(grad_score, query_bf, (((0,), (0,)), ((), ())), preferred_element_type=jnp.float32)
    return (conj_times(grad_query, rel_rows), grad_dst, grad_neg, conj_times(grad_query, source))

def row_adagrad(params, state, grad):
    new_state = state + lax.optimization_barrier(jnp.mean(grad * grad, axis=-1))
    return (params - LEARN_RATE * grad / (jnp.sqrt(new_state) + EPSILON)[:, None], new_state)

def plain_adagrad(params, state, grad):
    new_state = state + grad * grad
    return (params - LEARN_RATE * grad / (jnp.sqrt(new_state) + EPSILON), new_state)

def reference(embeddings, emb_state, relations, rel_state, matching, src_index, dst_index, rel_index, neg_index, counts):
    positions = jnp.arange(GROUP, dtype=jnp.int32)
    for round_id in range(ROUNDS):
        partners = jnp.bitwise_xor(jnp.arange(N_DOM, dtype=jnp.int32), matching[round_id])
        src_round = src_index[round_id]
        dst_round = dst_index[round_id]
        rel_round = rel_index[round_id]
        neg_round = neg_index[round_id]
        count_round = counts[round_id]

        def one_bucket(carry, bucket):
            grad_all, grad_rel = carry
            owner_base = bucket * ROWS
            partner_base = partners[bucket] * ROWS
            for group_id in range(GROUPS):
                first_edge = (bucket * CAP + group_id * GROUP).astype(jnp.int32)
                src_ids = lax.dynamic_slice_in_dim(src_round, first_edge, GROUP) + owner_base
                dst_ids = lax.dynamic_slice_in_dim(dst_round, first_edge, GROUP) + partner_base
                rel_ids = lax.dynamic_slice_in_dim(rel_round, first_edge, GROUP)
                first_neg = ((bucket * GROUPS + group_id) * NEG).astype(jnp.int32)
                neg_ids = lax.dynamic_slice_in_dim(neg_round, first_neg, NEG) + partner_base
                live_edge = (group_id * GROUP + positions < count_round[bucket]).astype(jnp.float32)
                src_bf = embeddings[src_ids].astype(jnp.bfloat16)
                dst_bf = embeddings[dst_ids].astype(jnp.bfloat16)
                neg_bf = embeddings[neg_ids].astype(jnp.bfloat16)
                grad_src, grad_dst, grad_neg, grad_relation = group_terms(src_bf, dst_bf, neg_bf, relations[rel_ids], live_edge)
                grad_all = grad_all.at[src_ids].add(grad_src).at[dst_ids].add(grad_dst).at[neg_ids].add(grad_neg)
                grad_rel = grad_rel.at[rel_ids].add(grad_relation)
            return ((grad_all, grad_rel), None)
        start_carry = (jnp.zeros(embeddings.shape, jnp.float32), jnp.zeros(relations.shape, jnp.float32))
        (grad_all, grad_rel), _ = lax.scan(one_bucket, start_carry, jnp.arange(N_DOM, dtype=jnp.int32))
        embeddings, emb_state = row_adagrad(embeddings, emb_state, grad_all)
        relations, rel_state = plain_adagrad(relations, rel_state, grad_rel)
    return (embeddings, emb_state, relations, rel_state)
```

```python
import functools

import jax
import jax.numpy as jnp
from jax import lax
from jax.experimental import pallas as pl
from jax.experimental.pallas import tpu as pltpu
from jax.sharding import PartitionSpec as P

ROUNDS = 2
LANES = 128
LEARN_RATE = 0.1
EPSILON = 1e-06
DIGIT_BITS = 5
MAX_OWNERS = 16
MESH = pl.DeviceIdType.MESH
BF = jnp.bfloat16
F32 = jnp.float32


def digits_of(count):
    out, stride = [], 1
    while stride < count:
        size = min(2**DIGIT_BITS, count // stride)
        out.append((stride, size))
        stride *= size
    return out


def nt(a, b):
    return lax.dot_general(a, b, (((1,), (1,)), ((), ())), preferred_element_type=F32)


def nn(a, b):
    return lax.dot_general(a, b, (((1,), (0,)), ((), ())), preferred_element_type=F32)


def tn(a, b):
    return lax.dot_general(a, b, (((0,), (0,)), ((), ())), preferred_element_type=F32)


def split(x):
    high = x.astype(BF)
    return high, (x - high.astype(F32)).astype(BF)


def one_hot(row, size):
    place = lax.broadcasted_iota(jnp.int32, (size, row.shape[1]), 0)
    return jnp.where(place == row, 1.0, 0.0).astype(BF)


def identity_mask():
    shape = (LANES, LANES)
    return lax.broadcasted_iota(jnp.int32, shape, 0) == lax.broadcasted_iota(jnp.int32, shape, 1)


def to_column(rows):
    eye = identity_mask()
    parts = [
        jnp.sum(jnp.where(eye, rows[b : b + 1, :], 0.0), axis=1, keepdims=True)
        for b in range(rows.shape[0])
    ]
    return jnp.concatenate(parts, axis=0)


def to_rows(column):
    eye = identity_mask()
    parts = [
        jnp.sum(
            jnp.where(eye, column[b * LANES : (b + 1) * LANES, :], 0.0), axis=0, keepdims=True
        )
        for b in range(column.shape[0] // LANES)
    ]
    return jnp.concatenate(parts, axis=0)


def put_halves(ref, value):
    rows, columns = value.shape
    for b in range(columns // LANES):
        ref[b * rows : (b + 1) * rows, :] = value[:, b * LANES : (b + 1) * LANES]


def get_halves(ref, rows):
    value = ref[...]
    return jnp.concatenate(
        [value[b * rows : (b + 1) * rows] for b in range(value.shape[0] // rows)], axis=1
    )


def kernel(
    count,
    owners,
    matching,
    counts,
    emb_in,
    state_in,
    rel_in,
    rstate_in,
    src_index,
    dst_index,
    rel_index,
    neg_index,
    emb,
    state,
    rel,
    rstate,
    meta,
    pay,
    first,
    stage,
    second,
    local,
    embt,
    onehot,
    relg,
    parts,
    total,
    send_sem,
    recv_sem,
    meta_send,
    meta_recv,
    part_send,
    part_recv,
    total_send,
    total_recv,
):
    digits = digits_of(count)
    me = lax.axis_index("dom")
    rows_count, width = emb_in.shape
    half = width // 2
    rel_count = rel_in.shape[0]
    slots = src_index.shape[1]
    negs = neg_index.shape[1]
    idx_rows, hist_rows = slots // LANES, rows_count // LANES
    part_rows = relg.shape[1] // owners
    owner_stride = count // owners
    is_owner = lax.rem(me, owner_stride) == 0

    def other(step):
        return lax.rem(me + step, count)

    barrier = pltpu.get_barrier_semaphore()

    def greet(step, carry):
        pl.semaphore_signal(barrier, inc=1, device_id=(other(step),), device_id_type=MESH)
        return carry

    lax.fori_loop(1, count, greet, 0)

    def send(source, target, send_at, recv_at, device):
        pltpu.make_async_remote_copy(
            src_ref=source,
            dst_ref=target,
            send_sem=send_at,
            recv_sem=recv_at,
            device_id=(device,),
            device_id_type=MESH,
        ).start()

    def await_bytes(view, sem):
        pltpu.make_async_copy(view, view, sem).wait()

    def place(j):
        stride, size = digits[j]
        return stride, size, lax.rem(lax.div(me, stride), size)

    def exchange_out(k, way, j, source):
        stride, size, mine = place(j)
        rows = first[j][0].shape[1]

        def piece(there):
            return source.at[pl.ds(pl.multiple_of(there * rows, rows), rows)]

        first[j][k * 2 + way][mine] = piece(mine)[...]

        def step(t, carry):
            there = lax.rem(mine + t, size)
            send(
                piece(there),
                first[j][k * 2 + way].at[mine],
                send_sem.at[k, way, j, 0],
                recv_sem.at[k, way, j, 0],
                me + (there - mine) * stride,
            )
            return carry

        lax.fori_loop(1, size, step, 0)

    def exchange_on(k, way, j):
        stride, size, mine = place(j)
        rows = first[j][0].shape[1]
        mask = matching[k]
        if len(digits) > 1:
            mask = lax.rem(lax.div(mask, stride), size)
        here = pl.ds(pl.multiple_of(mine * rows, rows), rows)
        await_bytes(first[j][k * 2 + way].at[pl.ds(0, size - 1)], recv_sem.at[k, way, j, 0])

        def step(t, carry):
            there = lax.rem(mine + t, size)
            stage[j][k * 2 + way, there] = first[j][k * 2 + way][jnp.bitwise_xor(there, mask)]
            send(
                stage[j].at[k * 2 + way, there],
                second.at[k, way, j, here],
                send_sem.at[k, way, j, 1],
                recv_sem.at[k, way, j, 1],
                me + (there - mine) * stride,
            )
            return carry

        lax.fori_loop(1, size, step, 0)
        second[k, way, j, here, :] = first[j][k * 2 + way][jnp.bitwise_xor(mine, mask)]

    def exchange_in(k, way, j):
        _, size = digits[j]
        rows = first[j][0].shape[1]
        await_bytes(second.at[k, way, j, pl.ds(0, (size - 1) * rows)], recv_sem.at[k, way, j, 1])

    def exchange_rest(k, way):
        exchange_in(k, way, 0)
        for j in range(1, len(digits)):
            exchange_out(k, way, j, second.at[k, way, j - 1])
            exchange_on(k, way, j)
            exchange_in(k, way, j)

    def make_meta(k):
        number = lax.broadcasted_iota(jnp.int32, (1, slots), 1)
        marked = jnp.where(number < counts[k, 0], rel_index[k : k + 1, :], -1)
        negative = neg_index[k : k + 1, :]
        low = one_hot(jnp.bitwise_and(negative, LANES - 1), LANES)
        high = one_hot(jnp.right_shift(negative, 7), max(8, hist_rows))
        times = nt(high, low)[:hist_rows].astype(jnp.int32)
        dst = dst_index[k : k + 1, :]
        rows = [dst[:, b * LANES : (b + 1) * LANES] for b in range(idx_rows)]
        rows += [marked[:, b * LANES : (b + 1) * LANES] for b in range(idx_rows)]
        meta[k][me] = jnp.concatenate(rows + [times], axis=0)

    def send_meta(k):
        def step(t, carry):
            send(meta[k].at[me], meta[k].at[me], meta_send.at[k], meta_recv.at[k], other(t))
            return carry

        lax.fori_loop(1, count, step, 0)

    def gather_sources(k):
        values = emb_in[...] if k == 0 else emb[...]
        turned = values.T.astype(BF)
        embt[k] = turned
        chosen = one_hot(src_index[k : k + 1, :], rows_count)
        onehot[k] = chosen
        put_halves(pay.at[k, 0], nn(turned, chosen).astype(BF))

    def work(k):
        relations = rel_in[...] if k == 0 else rel[...]
        values = (emb_in[...] if k == 0 else emb[...]).astype(BF)
        source = get_halves(second.at[k, 0, len(digits) - 1], width).astype(F32)
        await_bytes(meta[k].at[pl.ds(0, count - 1)], meta_recv.at[k])
        info = meta[k][jnp.bitwise_xor(me, matching[k])]
        dst_row = jnp.concatenate([info[b : b + 1] for b in range(idx_rows)], axis=1)
        rel_row = jnp.concatenate(
            [info[b : b + 1] for b in range(idx_rows, 2 * idx_rows)], axis=1
        )
        times = to_column(info[2 * idx_rows : 2 * idx_rows + hist_rows].astype(F32))
        live = jnp.where(rel_row >= 0, 1.0, 0.0)
        dst_hot = one_hot(dst_row, rows_count)
        rel_hot = one_hot(rel_row, rel_count)
        target = nn(embt[k], dst_hot)
        rel_high, rel_low = split(relations)
        factor = tn(rel_high, rel_hot) + tn(rel_low, rel_hot)
        s_re, s_im = source[:half], source[half:]
        r_re, r_im = factor[:half], factor[half:]
        query = jnp.concatenate([s_re * r_re - s_im * r_im, s_re * r_im + s_im * r_re], axis=0)
        positive = jnp.sum(query * target, axis=0, keepdims=True)
        query_b = query.astype(BF)
        scores = nn(values, query_b)
        weights = (jax.nn.sigmoid(scores) * (times * (1.0 / negs)) * live).astype(BF)
        grad_pos = -jax.nn.sigmoid(-positive) * live
        grad_query = grad_pos * target + nn(embt[k], weights)
        g_re, g_im = grad_query[:half], grad_query[half:]
        put_halves(
            pay.at[k, 1],
            jnp.concatenate([g_re * r_re + g_im * r_im, g_im * r_re - g_re * r_im], axis=0).astype(
                BF
            ),
        )
        exchange_out(k, 1, 0, pay.at[k, 1])
        rel_high, rel_low = split(
            jnp.concatenate([g_re * s_re + g_im * s_im, g_im * s_re - g_re * s_im], axis=0)
        )
        put_halves(relg.at[k], nt(rel_hot, rel_high) + nt(rel_hot, rel_low))
        send_parts(k)
        dst_high, dst_low = split(grad_pos * query)
        local[...] = nt(weights, query_b) + nt(dst_hot, dst_high) + nt(dst_hot, dst_low)

    my_part = pl.ds(pl.multiple_of(me * part_rows, part_rows), part_rows)
    owner = lax.div(me, owner_stride)
    owned = pl.ds(pl.multiple_of(owner * part_rows, part_rows), part_rows)

    def send_parts(k):
        def step(o, carry):
            device = o * owner_stride

            @pl.when(device != me)
            def _():
                send(
                    relg.at[k, pl.ds(pl.multiple_of(o * part_rows, part_rows), part_rows)],
                    parts.at[k, my_part],
                    part_send.at[k],
                    part_recv.at[k],
                    device,
                )

            return carry

        lax.fori_loop(0, owners, step, 0)

        @pl.when(is_owner)
        def _():
            parts[k, my_part, :] = relg[k, owned, :]

    def add_parts(k):
        @pl.when(is_owner)
        def _():
            await_bytes(parts.at[k, pl.ds(0, (count - 1) * part_rows)], part_recv.at[k])
            added = parts[k].reshape(count, part_rows, LANES)
            total[k, owned, :] = jnp.sum(added, axis=0)

            def step(t, carry):
                send(
                    total.at[k, owned],
                    total.at[k, owned],
                    total_send.at[k],
                    total_recv.at[k],
                    other(t),
                )
                return carry

            lax.fori_loop(1, count, step, 0)

    def update_relations(k):
        @pl.when(is_owner)
        def _():
            await_bytes(total.at[k, pl.ds(0, (owners - 1) * part_rows)], total_recv.at[k])

        if owners < count:

            @pl.when(jnp.logical_not(is_owner))
            def _():
                await_bytes(total.at[k], total_recv.at[k])

        grad = get_halves(total.at[k], rel_count)
        new_state = (rstate_in[...] if k == 0 else rstate[...]) + grad * grad
        rstate[...] = new_state
        rel[...] = (rel_in[...] if k == 0 else rel[...]) - LEARN_RATE * grad / (
            jnp.sqrt(new_state) + EPSILON
        )

    def update_entities(k):
        returned = get_halves(second.at[k, 1, len(digits) - 1], width)
        grad = local[...] + nt(onehot[k], returned)
        old_state = to_column(state_in[...] if k == 0 else state[...])
        new_state = old_state + jnp.sum(grad * grad, axis=1, keepdims=True) * (1.0 / width)
        state[...] = to_rows(new_state)
        emb[...] = (emb_in[...] if k == 0 else emb[...]) - grad * (
            LEARN_RATE / (jnp.sqrt(new_state) + EPSILON)
        )

    gather_sources(0)
    make_meta(0)
    pl.semaphore_wait(barrier, count - 1)
    exchange_out(0, 0, 0, pay.at[0, 0])
    send_meta(0)
    for k in range(ROUNDS):
        exchange_on(k, 0, 0)
        if k + 1 < ROUNDS:
            make_meta(k + 1)
        if k > 0:
            update_relations(k - 1)
        exchange_rest(k, 0)
        work(k)
        exchange_on(k, 1, 0)
        if k + 1 < ROUNDS:
            send_meta(k + 1)
        add_parts(k)
        exchange_rest(k, 1)
        update_entities(k)
        if k + 1 < ROUNDS:
            gather_sources(k + 1)
            exchange_out(k + 1, 0, 0, pay.at[k + 1, 0])
    update_relations(ROUNDS - 1)

    for k in range(ROUNDS):
        for way in range(2):
            for j in range(len(digits)):
                _, size = digits[j]
                for phase in range(2):
                    view = stage[j].at[k * 2 + way, pl.ds(0, size - 1)]
                    await_bytes(view, send_sem.at[k, way, j, phase])
        await_bytes(meta[k].at[pl.ds(0, count - 1)], meta_send.at[k])

        @pl.when(is_owner)
        def _():
            await_bytes(relg.at[k, pl.ds(0, (owners - 1) * part_rows)], part_send.at[k])
            await_bytes(parts.at[k, pl.ds(0, (count - 1) * part_rows)], total_send.at[k])

        if owners < count:

            @pl.when(jnp.logical_not(is_owner))
            def _():
                await_bytes(relg.at[k], part_send.at[k])


def on_device(count, embeddings, emb_state, relations, rel_state, matching, *lists):
    src_index, dst_index, rel_index, neg_index, counts = lists
    rows_count, width = embeddings.shape
    slots = src_index.shape[1]
    rel_count = relations.shape[0]
    digits = len(digits_of(count))
    owners = min(MAX_OWNERS, count)
    pay_rows = width * (slots // LANES)
    meta_rows = 2 * (slots // LANES) + rows_count // LANES
    rel_rows = rel_count * (width // LANES)
    vmem, smem = (pl.BlockSpec(memory_space=space) for space in (pltpu.VMEM, pltpu.SMEM))
    dma = pltpu.SemaphoreType.DMA
    pieces = tuple(
        pltpu.VMEM((ROUNDS * 2, size, pay_rows // size, LANES), BF)
        for _, size in digits_of(count)
    )
    arriving = tuple(
        (pltpu.VMEM((size, pay_rows // size, LANES), BF),) * (ROUNDS * 2)
        for _, size in digits_of(count)
    )
    out = pl.pallas_call(
        functools.partial(kernel, count, owners),
        out_shape=(
            jax.ShapeDtypeStruct((rows_count, width), F32),
            jax.ShapeDtypeStruct((rows_count // LANES, LANES), F32),
            jax.ShapeDtypeStruct((rel_count, width), F32),
            jax.ShapeDtypeStruct((rel_count, width), F32),
        ),
        in_specs=[smem, smem] + [vmem] * 8,
        out_specs=(vmem,) * 4,
        scratch_shapes=[
            (pltpu.VMEM((count, meta_rows, LANES), jnp.int32),) * ROUNDS,
            pltpu.VMEM((ROUNDS, 2, pay_rows, LANES), BF),
            arriving,
            pieces,
            pltpu.VMEM((ROUNDS, 2, digits, pay_rows, LANES), BF),
            pltpu.VMEM((rows_count, width), F32),
            pltpu.VMEM((ROUNDS, width, rows_count), BF),
            pltpu.VMEM((ROUNDS, rows_count, slots), BF),
            pltpu.VMEM((ROUNDS, rel_rows, LANES), F32),
            pltpu.VMEM((ROUNDS, count * (rel_rows // owners), LANES), F32),
            pltpu.VMEM((ROUNDS, rel_rows, LANES), F32),
            dma((ROUNDS, 2, digits, 2)),
            dma((ROUNDS, 2, digits, 2)),
            dma((ROUNDS,)),
            dma((ROUNDS,)),
            dma((ROUNDS,)),
            dma((ROUNDS,)),
            dma((ROUNDS,)),
            dma((ROUNDS,)),
        ],
        compiler_params=pltpu.CompilerParams(
            collective_id=0, has_side_effects=True, vmem_limit_bytes=40 * 2**20
        ),
    )(
        matching,
        counts,
        embeddings,
        emb_state.reshape(rows_count // LANES, LANES),
        relations,
        rel_state,
        src_index,
        dst_index,
        rel_index,
        neg_index,
    )
    return out[0], out[1].reshape(rows_count), out[2], out[3]


def solution(mesh):
    return jax.shard_map(
        functools.partial(on_device, mesh.shape["dom"]),
        mesh=mesh,
        in_specs=(
            P("dom", None),
            P("dom"),
            P(),
            P(),
            P(),
            P(None, "dom"),
            P(None, "dom"),
            P(None, "dom"),
            P(None, "dom"),
            P(None, "dom"),
        ),
        out_specs=(P("dom", None), P("dom"), P(), P()),
        check_vma=False,
    )
```

```python
import functools

import jax
import jax.numpy as jnp
from jax import lax
from jax.experimental import pallas as pl
from jax.experimental.pallas import tpu as pltpu
from jax.sharding import PartitionSpec as P

ROUNDS = 2
LANES = 128
LEARN_RATE = 0.1
EPSILON = 1e-06
DIGIT_BITS = 5
MAX_OWNERS = 16
MESH = pl.DeviceIdType.MESH
BF = jnp.bfloat16
F32 = jnp.float32


def digits_of(count):
    out, stride = [], 1
    while stride < count:
        size = min(2**DIGIT_BITS, count // stride)
        out.append((stride, size))
        stride *= size
    return out


def nt(a, b):
    return lax.dot_general(a, b, (((1,), (1,)), ((), ())), preferred_element_type=F32)


def nn(a, b):
    return lax.dot_general(a, b, (((1,), (0,)), ((), ())), preferred_element_type=F32)


def tn(a, b):
    return lax.dot_general(a, b, (((0,), (0,)), ((), ())), preferred_element_type=F32)


def split(x):
    high = x.astype(BF)
    return high, (x - high.astype(F32)).astype(BF)


def one_hot(row, size):
    place = lax.broadcasted_iota(jnp.int32, (size, row.shape[1]), 0)
    return jnp.where(place == row, 1.0, 0.0).astype(BF)


def identity_mask():
    shape = (LANES, LANES)
    return lax.broadcasted_iota(jnp.int32, shape, 0) == lax.broadcasted_iota(jnp.int32, shape, 1)


def to_column(rows):
    eye = identity_mask()
    parts = [
        jnp.sum(jnp.where(eye, rows[b : b + 1, :], 0.0), axis=1, keepdims=True)
        for b in range(rows.shape[0])
    ]
    return jnp.concatenate(parts, axis=0)


def to_rows(column):
    eye = identity_mask()
    parts = [
        jnp.sum(
            jnp.where(eye, column[b * LANES : (b + 1) * LANES, :], 0.0), axis=0, keepdims=True
        )
        for b in range(column.shape[0] // LANES)
    ]
    return jnp.concatenate(parts, axis=0)


def put_halves(ref, value):
    rows, columns = value.shape
    for b in range(columns // LANES):
        ref[b * rows : (b + 1) * rows, :] = value[:, b * LANES : (b + 1) * LANES]


def get_halves(ref, rows):
    value = ref[...]
    return jnp.concatenate(
        [value[b * rows : (b + 1) * rows] for b in range(value.shape[0] // rows)], axis=1
    )


def kernel(
    count,
    owners,
    matching,
    counts,
    emb_arg,
    state_arg,
    rel_arg,
    rstate_arg,
    src_arg,
    dst_arg,
    rel_index_arg,
    neg_arg,
    emb,
    state,
    rel,
    rstate,
    emb_in,
    state_in,
    rel_in,
    rstate_in,
    src_index,
    dst_index,
    rel_index,
    neg_index,
    meta,
    pay,
    first,
    stage,
    second,
    local,
    embt,
    onehot,
    relg,
    parts,
    total,
    send_sem,
    recv_sem,
    meta_send,
    meta_recv,
    part_send,
    part_recv,
    total_send,
    total_recv,
    load_sem,
):
    loads = [
        pltpu.make_async_copy(source, target, load_sem.at[i])
        for i, (source, target) in enumerate(
            (
                (emb_arg, emb_in),
                (src_arg, src_index),
                (neg_arg, neg_index),
                (dst_arg, dst_index),
                (rel_index_arg, rel_index),
                (state_arg, state_in),
                (rel_arg, rel_in),
                (rstate_arg, rstate_in),
            )
        )
    ]
    for load in loads:
        load.start()
    digits = digits_of(count)
    me = lax.axis_index("dom")
    rows_count, width = emb_in.shape
    half = width // 2
    rel_count = rel_in.shape[0]
    slots = src_index.shape[1]
    negs = neg_index.shape[1]
    idx_rows, hist_rows = slots // LANES, rows_count // LANES
    part_rows = relg.shape[1] // owners
    owner_stride = count // owners
    is_owner = lax.rem(me, owner_stride) == 0

    def other(step):
        return lax.rem(me + step, count)

    barrier = pltpu.get_barrier_semaphore()

    def greet(step, carry):
        pl.semaphore_signal(barrier, inc=1, device_id=(other(step),), device_id_type=MESH)
        return carry

    lax.fori_loop(1, count, greet, 0)

    def send(source, target, send_at, recv_at, device):
        pltpu.make_async_remote_copy(
            src_ref=source,
            dst_ref=target,
            send_sem=send_at,
            recv_sem=recv_at,
            device_id=(device,),
            device_id_type=MESH,
        ).start()

    def await_bytes(view, sem):
        pltpu.make_async_copy(view, view, sem).wait()

    def place(j):
        stride, size = digits[j]
        return stride, size, lax.rem(lax.div(me, stride), size)

    def exchange_out(k, way, j, source):
        stride, size, mine = place(j)
        rows = first[j][0].shape[1]

        def piece(there):
            return source.at[pl.ds(pl.multiple_of(there * rows, rows), rows)]

        first[j][k * 2 + way][mine] = piece(mine)[...]

        def step(t, carry):
            there = lax.rem(mine + t, size)
            send(
                piece(there),
                first[j][k * 2 + way].at[mine],
                send_sem.at[k, way, j, 0],
                recv_sem.at[k, way, j, 0],
                me + (there - mine) * stride,
            )
            return carry

        lax.fori_loop(1, size, step, 0)

    def exchange_on(k, way, j):
        stride, size, mine = place(j)
        rows = first[j][0].shape[1]
        mask = matching[k]
        if len(digits) > 1:
            mask = lax.rem(lax.div(mask, stride), size)
        here = pl.ds(pl.multiple_of(mine * rows, rows), rows)
        await_bytes(first[j][k * 2 + way].at[pl.ds(0, size - 1)], recv_sem.at[k, way, j, 0])

        def step(t, carry):
            there = lax.rem(mine + t, size)
            stage[j][k * 2 + way, there] = first[j][k * 2 + way][jnp.bitwise_xor(there, mask)]
            send(
                stage[j].at[k * 2 + way, there],
                second.at[k, way, j, here],
                send_sem.at[k, way, j, 1],
                recv_sem.at[k, way, j, 1],
                me + (there - mine) * stride,
            )
            return carry

        lax.fori_loop(1, size, step, 0)
        second[k, way, j, here, :] = first[j][k * 2 + way][jnp.bitwise_xor(mine, mask)]

    def exchange_in(k, way, j):
        _, size = digits[j]
        rows = first[j][0].shape[1]
        await_bytes(second.at[k, way, j, pl.ds(0, (size - 1) * rows)], recv_sem.at[k, way, j, 1])

    def exchange_rest(k, way):
        exchange_in(k, way, 0)
        for j in range(1, len(digits)):
            exchange_out(k, way, j, second.at[k, way, j - 1])
            exchange_on(k, way, j)
            exchange_in(k, way, j)

    def make_meta(k):
        number = lax.broadcasted_iota(jnp.int32, (1, slots), 1)
        marked = jnp.where(number < counts[k], rel_index[k : k + 1, :], -1)
        negative = neg_index[k : k + 1, :]
        low = one_hot(jnp.bitwise_and(negative, LANES - 1), LANES)
        high = one_hot(jnp.right_shift(negative, 7), max(8, hist_rows))
        times = nt(high, low)[:hist_rows].astype(jnp.int32)
        dst = dst_index[k : k + 1, :]
        rows = [dst[:, b * LANES : (b + 1) * LANES] for b in range(idx_rows)]
        rows += [marked[:, b * LANES : (b + 1) * LANES] for b in range(idx_rows)]
        meta[k][me] = jnp.concatenate(rows + [times], axis=0)

    def send_meta(k):
        def step(t, carry):
            send(meta[k].at[me], meta[k].at[me], meta_send.at[k], meta_recv.at[k], other(t))
            return carry

        lax.fori_loop(1, count, step, 0)

    def gather_sources(k):
        values = emb_in[...] if k == 0 else emb[...]
        turned = values.T.astype(BF)
        embt[k] = turned
        chosen = one_hot(src_index[k : k + 1, :], rows_count)
        onehot[k] = chosen
        put_halves(pay.at[k, 0], nn(turned, chosen).astype(BF))

    def work(k):
        relations = rel_in[...] if k == 0 else rel[...]
        values = (emb_in[...] if k == 0 else emb[...]).astype(BF)
        source = get_halves(second.at[k, 0, len(digits) - 1], width).astype(F32)
        await_bytes(meta[k].at[pl.ds(0, count - 1)], meta_recv.at[k])
        info = meta[k][jnp.bitwise_xor(me, matching[k])]
        dst_row = jnp.concatenate([info[b : b + 1] for b in range(idx_rows)], axis=1)
        rel_row = jnp.concatenate(
            [info[b : b + 1] for b in range(idx_rows, 2 * idx_rows)], axis=1
        )
        times = to_column(info[2 * idx_rows : 2 * idx_rows + hist_rows].astype(F32))
        live = jnp.where(rel_row >= 0, 1.0, 0.0)
        dst_hot = one_hot(dst_row, rows_count)
        rel_hot = one_hot(rel_row, rel_count)
        target = nn(embt[k], dst_hot)
        rel_high, rel_low = split(relations)
        factor = tn(rel_high, rel_hot) + tn(rel_low, rel_hot)
        s_re, s_im = source[:half], source[half:]
        r_re, r_im = factor[:half], factor[half:]
        query = jnp.concatenate([s_re * r_re - s_im * r_im, s_re * r_im + s_im * r_re], axis=0)
        positive = jnp.sum(query * target, axis=0, keepdims=True)
        query_b = query.astype(BF)
        scores = nn(values, query_b)
        weights = (jax.nn.sigmoid(scores) * (times * (1.0 / negs)) * live).astype(BF)
        grad_pos = -jax.nn.sigmoid(-positive) * live
        grad_query = grad_pos * target + nn(embt[k], weights)
        g_re, g_im = grad_query[:half], grad_query[half:]
        put_halves(
            pay.at[k, 1],
            jnp.concatenate([g_re * r_re + g_im * r_im, g_im * r_re - g_re * r_im], axis=0).astype(
                BF
            ),
        )
        exchange_out(k, 1, 0, pay.at[k, 1])
        rel_high, rel_low = split(
            jnp.concatenate([g_re * s_re + g_im * s_im, g_im * s_re - g_re * s_im], axis=0)
        )
        put_halves(relg.at[k], nt(rel_hot, rel_high) + nt(rel_hot, rel_low))
        send_parts(k)
        dst_high, dst_low = split(grad_pos * query)
        local[...] = nt(weights, query_b) + nt(dst_hot, dst_high) + nt(dst_hot, dst_low)

    my_part = pl.ds(pl.multiple_of(me * part_rows, part_rows), part_rows)
    owner = lax.div(me, owner_stride)
    owned = pl.ds(pl.multiple_of(owner * part_rows, part_rows), part_rows)

    def send_parts(k):
        def step(o, carry):
            device = o * owner_stride

            @pl.when(device != me)
            def _():
                send(
                    relg.at[k, pl.ds(pl.multiple_of(o * part_rows, part_rows), part_rows)],
                    parts.at[k, my_part],
                    part_send.at[k],
                    part_recv.at[k],
                    device,
                )

            return carry

        lax.fori_loop(0, owners, step, 0)

        @pl.when(is_owner)
        def _():
            parts[k, my_part, :] = relg[k, owned, :]

    def add_parts(k):
        @pl.when(is_owner)
        def _():
            await_bytes(parts.at[k, pl.ds(0, (count - 1) * part_rows)], part_recv.at[k])
            added = parts[k].reshape(count, part_rows, LANES)
            total[k, owned, :] = jnp.sum(added, axis=0)

            def step(t, carry):
                send(
                    total.at[k, owned],
                    total.at[k, owned],
                    total_send.at[k],
                    total_recv.at[k],
                    other(t),
                )
                return carry

            lax.fori_loop(1, count, step, 0)

    def update_relations(k):
        @pl.when(is_owner)
        def _():
            await_bytes(total.at[k, pl.ds(0, (owners - 1) * part_rows)], total_recv.at[k])

        if owners < count:

            @pl.when(jnp.logical_not(is_owner))
            def _():
                await_bytes(total.at[k], total_recv.at[k])

        grad = get_halves(total.at[k], rel_count)
        new_state = (rstate_in[...] if k == 0 else rstate[...]) + grad * grad
        rstate[...] = new_state
        rel[...] = (rel_in[...] if k == 0 else rel[...]) - LEARN_RATE * grad / (
            jnp.sqrt(new_state) + EPSILON
        )

    def update_entities(k):
        returned = get_halves(second.at[k, 1, len(digits) - 1], width)
        grad = local[...] + nt(onehot[k], returned)
        old_state = to_column(state_in[...] if k == 0 else state[...])
        new_state = old_state + jnp.sum(grad * grad, axis=1, keepdims=True) * (1.0 / width)
        state[...] = to_rows(new_state)
        emb[...] = (emb_in[...] if k == 0 else emb[...]) - grad * (
            LEARN_RATE / (jnp.sqrt(new_state) + EPSILON)
        )

    loads[0].wait()
    loads[1].wait()
    gather_sources(0)
    for load in loads[2:]:
        load.wait()
    make_meta(0)
    pl.semaphore_wait(barrier, count - 1)
    exchange_out(0, 0, 0, pay.at[0, 0])
    send_meta(0)
    for k in range(ROUNDS):
        exchange_on(k, 0, 0)
        if k + 1 < ROUNDS:
            make_meta(k + 1)
        if k > 0:
            update_relations(k - 1)
        exchange_rest(k, 0)
        work(k)
        exchange_on(k, 1, 0)
        if k + 1 < ROUNDS:
            send_meta(k + 1)
        add_parts(k)
        exchange_rest(k, 1)
        update_entities(k)
        if k + 1 < ROUNDS:
            gather_sources(k + 1)
            exchange_out(k + 1, 0, 0, pay.at[k + 1, 0])
    update_relations(ROUNDS - 1)

    for k in range(ROUNDS):
        for way in range(2):
            for j in range(len(digits)):
                _, size = digits[j]
                for phase in range(2):
                    view = stage[j].at[k * 2 + way, pl.ds(0, size - 1)]
                    await_bytes(view, send_sem.at[k, way, j, phase])
        await_bytes(meta[k].at[pl.ds(0, count - 1)], meta_send.at[k])

        @pl.when(is_owner)
        def _():
            await_bytes(relg.at[k, pl.ds(0, (owners - 1) * part_rows)], part_send.at[k])
            await_bytes(parts.at[k, pl.ds(0, (count - 1) * part_rows)], total_send.at[k])

        if owners < count:

            @pl.when(jnp.logical_not(is_owner))
            def _():
                await_bytes(relg.at[k], part_send.at[k])


def store(*refs):
    copies = [pltpu.make_async_copy(refs[i], refs[4 + i], refs[8].at[i]) for i in range(4)]
    for copy in copies:
        copy.start()
    for copy in copies:
        copy.wait()


def on_device(count, embeddings, emb_state, relations, rel_state, matching, *lists):
    src_index, dst_index, rel_index, neg_index, counts = lists
    rows_count, width = embeddings.shape
    slots = src_index.shape[1]
    rel_count = relations.shape[0]
    digits = len(digits_of(count))
    owners = min(MAX_OWNERS, count)
    pay_rows = width * (slots // LANES)
    meta_rows = 2 * (slots // LANES) + rows_count // LANES
    rel_rows = rel_count * (width // LANES)
    vmem, smem = (pl.BlockSpec(memory_space=space) for space in (pltpu.VMEM, pltpu.SMEM))
    dma = pltpu.SemaphoreType.DMA
    pieces = tuple(
        pltpu.VMEM((ROUNDS * 2, size, pay_rows // size, LANES), BF)
        for _, size in digits_of(count)
    )
    arriving = tuple(
        (pltpu.VMEM((size, pay_rows // size, LANES), BF),) * (ROUNDS * 2)
        for _, size in digits_of(count)
    )
    out = pl.pallas_call(
        functools.partial(kernel, count, owners),
        out_shape=(
            jax.ShapeDtypeStruct((rows_count, width), F32),
            jax.ShapeDtypeStruct((rows_count // LANES, LANES), F32),
            jax.ShapeDtypeStruct((rel_count, width), F32),
            jax.ShapeDtypeStruct((rel_count, width), F32),
        ),
        in_specs=[smem, smem] + [pl.BlockSpec(memory_space=pltpu.HBM)] * 8,
        out_specs=(vmem,) * 4,
        scratch_shapes=[
            pltpu.VMEM((rows_count, width), F32),
            pltpu.VMEM((rows_count // LANES, LANES), F32),
            pltpu.VMEM((rel_count, width), F32),
            pltpu.VMEM((rel_count, width), F32),
            pltpu.VMEM(src_index.shape, jnp.int32),
            pltpu.VMEM(dst_index.shape, jnp.int32),
            pltpu.VMEM(rel_index.shape, jnp.int32),
            pltpu.VMEM(neg_index.shape, jnp.int32),
            (pltpu.VMEM((count, meta_rows, LANES), jnp.int32),) * ROUNDS,
            pltpu.VMEM((ROUNDS, 2, pay_rows, LANES), BF),
            arriving,
            pieces,
            pltpu.VMEM((ROUNDS, 2, digits, pay_rows, LANES), BF),
            pltpu.VMEM((rows_count, width), F32),
            pltpu.VMEM((ROUNDS, width, rows_count), BF),
            pltpu.VMEM((ROUNDS, rows_count, slots), BF),
            pltpu.VMEM((ROUNDS, rel_rows, LANES), F32),
            pltpu.VMEM((ROUNDS, count * (rel_rows // owners), LANES), F32),
            pltpu.VMEM((ROUNDS, rel_rows, LANES), F32),
            dma((ROUNDS, 2, digits, 2)),
            dma((ROUNDS, 2, digits, 2)),
            dma((ROUNDS,)),
            dma((ROUNDS,)),
            dma((ROUNDS,)),
            dma((ROUNDS,)),
            dma((ROUNDS,)),
            dma((ROUNDS,)),
            dma((8,)),
        ],
        compiler_params=pltpu.CompilerParams(
            collective_id=0, has_side_effects=True, vmem_limit_bytes=62 * 2**20
        ),
    )(
        matching,
        counts.reshape(ROUNDS),
        embeddings,
        emb_state.reshape(rows_count // LANES, LANES),
        relations,
        rel_state,
        src_index,
        dst_index,
        rel_index,
        neg_index,
    )
    out = pl.pallas_call(
        store,
        out_shape=tuple(jax.ShapeDtypeStruct(x.shape, x.dtype) for x in out),
        in_specs=[vmem] * 4,
        out_specs=(pl.BlockSpec(memory_space=pltpu.HBM),) * 4,
        scratch_shapes=[dma((4,))],
    )(*out)
    return out[0], out[1].reshape(rows_count), out[2], out[3]


def solution(mesh):
    return jax.shard_map(
        functools.partial(on_device, mesh.shape["dom"]),
        mesh=mesh,
        in_specs=(
            P("dom", None),
            P("dom"),
            P(),
            P(),
            P(),
            P(None, "dom"),
            P(None, "dom"),
            P(None, "dom"),
            P(None, "dom"),
            P(None, "dom"),
        ),
        out_specs=(P("dom", None), P("dom"), P(), P()),
        check_vma=False,
    )
```

```python
import functools

import jax
import jax.numpy as jnp
from jax import lax
from jax.experimental import pallas as pl
from jax.experimental.pallas import tpu as pltpu
from jax.sharding import PartitionSpec as P

ROUNDS = 2
LANES = 128
LEARN_RATE = 0.1
EPSILON = 1e-06
DIGIT_BITS = 5
MAX_OWNERS = 16
MESH = pl.DeviceIdType.MESH
BF = jnp.bfloat16
F32 = jnp.float32


def digits_of(count):
    out, stride = [], 1
    while stride < count:
        size = min(2**DIGIT_BITS, count // stride)
        out.append((stride, size))
        stride *= size
    return out


def nt(a, b):
    return lax.dot_general(a, b, (((1,), (1,)), ((), ())), preferred_element_type=F32)


def nn(a, b):
    return lax.dot_general(a, b, (((1,), (0,)), ((), ())), preferred_element_type=F32)


def tn(a, b):
    return lax.dot_general(a, b, (((0,), (0,)), ((), ())), preferred_element_type=F32)


def split(x):
    high = x.astype(BF)
    return high, (x - high.astype(F32)).astype(BF)


def one_hot(row, size):
    place = lax.broadcasted_iota(jnp.int32, (size, row.shape[1]), 0)
    return jnp.where(place == row, 1.0, 0.0).astype(BF)


def identity_mask():
    shape = (LANES, LANES)
    return lax.broadcasted_iota(jnp.int32, shape, 0) == lax.broadcasted_iota(jnp.int32, shape, 1)


def to_column(rows):
    eye = identity_mask()
    parts = [
        jnp.sum(jnp.where(eye, rows[b : b + 1, :], 0.0), axis=1, keepdims=True)
        for b in range(rows.shape[0])
    ]
    return jnp.concatenate(parts, axis=0)


def to_rows(column):
    eye = identity_mask()
    parts = [
        jnp.sum(
            jnp.where(eye, column[b * LANES : (b + 1) * LANES, :], 0.0), axis=0, keepdims=True
        )
        for b in range(column.shape[0] // LANES)
    ]
    return jnp.concatenate(parts, axis=0)


def put_halves(ref, value):
    rows, columns = value.shape
    for b in range(columns // LANES):
        ref[b * rows : (b + 1) * rows, :] = value[:, b * LANES : (b + 1) * LANES]


def get_halves(ref, rows):
    value = ref[...]
    return jnp.concatenate(
        [value[b * rows : (b + 1) * rows] for b in range(value.shape[0] // rows)], axis=1
    )


def kernel(
    count,
    owners,
    matching,
    counts,
    emb_arg,
    state_arg,
    rel_arg,
    rstate_arg,
    src_arg,
    dst_arg,
    rel_index_arg,
    neg_arg,
    emb,
    state,
    rel,
    rstate,
    emb_in,
    state_in,
    rel_in,
    rstate_in,
    src_index,
    dst_index,
    rel_index,
    neg_index,
    meta,
    pay,
    first,
    stage,
    second,
    local,
    embt,
    onehot,
    relg,
    parts,
    total,
    send_sem,
    recv_sem,
    meta_send,
    meta_recv,
    part_send,
    part_recv,
    total_send,
    total_recv,
    load_sem,
):
    loads = [
        pltpu.make_async_copy(source, target, load_sem.at[i])
        for i, (source, target) in enumerate(
            (
                (emb_arg, emb_in),
                (src_arg, src_index),
                (neg_arg, neg_index),
                (dst_arg, dst_index),
                (rel_index_arg, rel_index),
                (state_arg, state_in),
                (rel_arg, rel_in),
                (rstate_arg, rstate_in),
            )
        )
    ]
    for load in loads:
        load.start()
    digits = digits_of(count)
    me = lax.axis_index("dom")
    rows_count, width = emb_in.shape
    half = width // 2
    rel_count = rel_in.shape[0]
    slots = src_index.shape[1]
    negs = neg_index.shape[1]
    idx_rows, hist_rows = slots // LANES, rows_count // LANES
    part_rows = relg.shape[1] // owners
    owner_stride = count // owners
    is_owner = lax.rem(me, owner_stride) == 0

    def other(step):
        return lax.rem(me + step, count)

    barrier = pltpu.get_barrier_semaphore()

    def greet(step, carry):
        pl.semaphore_signal(barrier, inc=1, device_id=(other(step),), device_id_type=MESH)
        return carry

    lax.fori_loop(1, count, greet, 0)

    def send(source, target, send_at, recv_at, device):
        pltpu.make_async_remote_copy(
            src_ref=source,
            dst_ref=target,
            send_sem=send_at,
            recv_sem=recv_at,
            device_id=(device,),
            device_id_type=MESH,
        ).start()

    def await_bytes(view, sem):
        pltpu.make_async_copy(view, view, sem).wait()

    def place(j):
        stride, size = digits[j]
        return stride, size, lax.rem(lax.div(me, stride), size)

    def exchange_out(k, way, j, source):
        stride, size, mine = place(j)
        rows = first[j][0].shape[1]

        def piece(there):
            return source.at[pl.ds(pl.multiple_of(there * rows, rows), rows)]

        first[j][k * 2 + way][mine] = piece(mine)[...]

        def step(t, carry):
            there = lax.rem(mine + t, size)
            send(
                piece(there),
                first[j][k * 2 + way].at[mine],
                send_sem.at[k, way, j, 0],
                recv_sem.at[k, way, j, 0],
                me + (there - mine) * stride,
            )
            return carry

        lax.fori_loop(1, size, step, 0)

    def exchange_on(k, way, j):
        stride, size, mine = place(j)
        rows = first[j][0].shape[1]
        mask = matching[k]
        if len(digits) > 1:
            mask = lax.rem(lax.div(mask, stride), size)
        here = pl.ds(pl.multiple_of(mine * rows, rows), rows)
        await_bytes(first[j][k * 2 + way].at[pl.ds(0, size - 1)], recv_sem.at[k, way, j, 0])

        def step(t, carry):
            there = lax.rem(mine + t, size)
            stage[j][k * 2 + way, there] = first[j][k * 2 + way][jnp.bitwise_xor(there, mask)]
            send(
                stage[j].at[k * 2 + way, there],
                second.at[k, way, j, here],
                send_sem.at[k, way, j, 1],
                recv_sem.at[k, way, j, 1],
                me + (there - mine) * stride,
            )
            return carry

        lax.fori_loop(1, size, step, 0)
        second[k, way, j, here, :] = first[j][k * 2 + way][jnp.bitwise_xor(mine, mask)]

    def exchange_in(k, way, j):
        _, size = digits[j]
        rows = first[j][0].shape[1]
        await_bytes(second.at[k, way, j, pl.ds(0, (size - 1) * rows)], recv_sem.at[k, way, j, 1])

    def exchange_rest(k, way):
        exchange_in(k, way, 0)
        for j in range(1, len(digits)):
            exchange_out(k, way, j, second.at[k, way, j - 1])
            exchange_on(k, way, j)
            exchange_in(k, way, j)

    def make_meta(k):
        number = lax.broadcasted_iota(jnp.int32, (1, slots), 1)
        marked = jnp.where(number < counts[k], rel_index[k : k + 1, :], -1)
        negative = neg_index[k : k + 1, :]
        low = one_hot(jnp.bitwise_and(negative, LANES - 1), LANES)
        high = one_hot(jnp.right_shift(negative, 7), max(8, hist_rows))
        times = nt(high, low)[:hist_rows].astype(jnp.int32)
        dst = dst_index[k : k + 1, :]
        rows = [dst[:, b * LANES : (b + 1) * LANES] for b in range(idx_rows)]
        rows += [marked[:, b * LANES : (b + 1) * LANES] for b in range(idx_rows)]
        meta[k][me] = jnp.concatenate(rows + [times], axis=0)

    def send_meta(k):
        def step(t, carry):
            send(meta[k].at[me], meta[k].at[me], meta_send.at[k], meta_recv.at[k], other(t))
            return carry

        lax.fori_loop(1, count, step, 0)

    def choose(k):
        onehot[k] = one_hot(src_index[k : k + 1, :], rows_count)

    def gather_sources(k):
        values = emb_in[...] if k == 0 else emb[...]
        turned = values.astype(BF).T
        embt[k] = turned
        put_halves(pay.at[k, 0], nn(turned, onehot[k]).astype(BF))

    def prepare(k):
        relations = rel_in[...] if k == 0 else rel[...]
        await_bytes(meta[k].at[pl.ds(0, count - 1)], meta_recv.at[k])
        info = meta[k][jnp.bitwise_xor(me, matching[k])]
        dst_row = jnp.concatenate([info[b : b + 1] for b in range(idx_rows)], axis=1)
        rel_row = jnp.concatenate(
            [info[b : b + 1] for b in range(idx_rows, 2 * idx_rows)], axis=1
        )
        times = to_column(info[2 * idx_rows : 2 * idx_rows + hist_rows].astype(F32))
        live = jnp.where(rel_row >= 0, 1.0, 0.0)
        dst_hot = one_hot(dst_row, rows_count)
        rel_hot = one_hot(rel_row, rel_count)
        target = nn(embt[k], dst_hot)
        rel_high, rel_low = split(relations)
        factor = tn(rel_high, rel_hot) + tn(rel_low, rel_hot)
        return target, factor, live, times * (1.0 / negs), dst_hot, rel_hot

    def work(k, target, factor, live, times, dst_hot, rel_hot):
        values = (emb_in[...] if k == 0 else emb[...]).astype(BF)
        source = get_halves(second.at[k, 0, len(digits) - 1], width).astype(F32)
        s_re, s_im = source[:half], source[half:]
        r_re, r_im = factor[:half], factor[half:]
        query = jnp.concatenate([s_re * r_re - s_im * r_im, s_re * r_im + s_im * r_re], axis=0)
        positive = jnp.sum(query * target, axis=0, keepdims=True)
        query_b = query.astype(BF)
        scores = nn(values, query_b)
        weights = (jax.nn.sigmoid(scores) * times * live).astype(BF)
        grad_pos = -jax.nn.sigmoid(-positive) * live
        grad_query = grad_pos * target + nn(embt[k], weights)
        g_re, g_im = grad_query[:half], grad_query[half:]
        put_halves(
            pay.at[k, 1],
            jnp.concatenate([g_re * r_re + g_im * r_im, g_im * r_re - g_re * r_im], axis=0).astype(
                BF
            ),
        )
        exchange_out(k, 1, 0, pay.at[k, 1])
        rel_high, rel_low = split(
            jnp.concatenate([g_re * s_re + g_im * s_im, g_im * s_re - g_re * s_im], axis=0)
        )
        put_halves(relg.at[k], nt(rel_hot, rel_high) + nt(rel_hot, rel_low))
        send_parts(k)
        dst_high, dst_low = split(grad_pos * query)
        local[...] = nt(weights, query_b) + nt(dst_hot, dst_high) + nt(dst_hot, dst_low)

    my_part = pl.ds(pl.multiple_of(me * part_rows, part_rows), part_rows)
    owner = lax.div(me, owner_stride)
    owned = pl.ds(pl.multiple_of(owner * part_rows, part_rows), part_rows)

    def send_parts(k):
        def step(o, carry):
            device = o * owner_stride

            @pl.when(device != me)
            def _():
                send(
                    relg.at[k, pl.ds(pl.multiple_of(o * part_rows, part_rows), part_rows)],
                    parts.at[k, my_part],
                    part_send.at[k],
                    part_recv.at[k],
                    device,
                )

            return carry

        lax.fori_loop(0, owners, step, 0)

        @pl.when(is_owner)
        def _():
            parts[k, my_part, :] = relg[k, owned, :]

    def add_parts(k):
        @pl.when(is_owner)
        def _():
            await_bytes(parts.at[k, pl.ds(0, (count - 1) * part_rows)], part_recv.at[k])
            added = parts[k].reshape(count, part_rows, LANES)
            total[k, owned, :] = jnp.sum(added, axis=0)

            def step(t, carry):
                send(
                    total.at[k, owned],
                    total.at[k, owned],
                    total_send.at[k],
                    total_recv.at[k],
                    other(t),
                )
                return carry

            lax.fori_loop(1, count, step, 0)

    def update_relations(k):
        @pl.when(is_owner)
        def _():
            await_bytes(total.at[k, pl.ds(0, (owners - 1) * part_rows)], total_recv.at[k])

        if owners < count:

            @pl.when(jnp.logical_not(is_owner))
            def _():
                await_bytes(total.at[k], total_recv.at[k])

        grad = get_halves(total.at[k], rel_count)
        new_state = (rstate_in[...] if k == 0 else rstate[...]) + grad * grad
        rstate[...] = new_state
        rel[...] = (rel_in[...] if k == 0 else rel[...]) - LEARN_RATE * grad / (
            jnp.sqrt(new_state) + EPSILON
        )

    def update_entities(k, old_state):
        returned = get_halves(second.at[k, 1, len(digits) - 1], width)
        grad = local[...] + nt(onehot[k], returned)
        new_state = old_state + jnp.sum(grad * grad, axis=1, keepdims=True) * (1.0 / width)
        state[...] = to_rows(new_state)
        emb[...] = (emb_in[...] if k == 0 else emb[...]) - grad * (
            LEARN_RATE / (jnp.sqrt(new_state) + EPSILON)
        )

    loads[0].wait()
    loads[1].wait()
    choose(0)
    gather_sources(0)
    for load in loads[2:]:
        load.wait()
    make_meta(0)
    pl.semaphore_wait(barrier, count - 1)
    exchange_out(0, 0, 0, pay.at[0, 0])
    send_meta(0)
    for k in range(ROUNDS):
        exchange_on(k, 0, 0)
        if k + 1 < ROUNDS:
            make_meta(k + 1)
            choose(k + 1)
        if k > 0:
            update_relations(k - 1)
        ready = prepare(k)
        exchange_rest(k, 0)
        work(k, *ready)
        exchange_on(k, 1, 0)
        if k + 1 < ROUNDS:
            send_meta(k + 1)
        add_parts(k)
        old_state = to_column(state_in[...] if k == 0 else state[...])
        exchange_rest(k, 1)
        update_entities(k, old_state)
        if k + 1 < ROUNDS:
            gather_sources(k + 1)
            exchange_out(k + 1, 0, 0, pay.at[k + 1, 0])
    update_relations(ROUNDS - 1)

    for k in range(ROUNDS):
        for way in range(2):
            for j in range(len(digits)):
                _, size = digits[j]
                for phase in range(2):
                    view = stage[j].at[k * 2 + way, pl.ds(0, size - 1)]
                    await_bytes(view, send_sem.at[k, way, j, phase])
        await_bytes(meta[k].at[pl.ds(0, count - 1)], meta_send.at[k])

        @pl.when(is_owner)
        def _():
            await_bytes(relg.at[k, pl.ds(0, (owners - 1) * part_rows)], part_send.at[k])
            await_bytes(parts.at[k, pl.ds(0, (count - 1) * part_rows)], total_send.at[k])

        if owners < count:

            @pl.when(jnp.logical_not(is_owner))
            def _():
                await_bytes(relg.at[k], part_send.at[k])


def store(*refs):
    copies = [pltpu.make_async_copy(refs[i], refs[4 + i], refs[8].at[i]) for i in range(4)]
    for copy in copies:
        copy.start()
    for copy in copies:
        copy.wait()


def on_device(count, embeddings, emb_state, relations, rel_state, matching, *lists):
    src_index, dst_index, rel_index, neg_index, counts = lists
    rows_count, width = embeddings.shape
    slots = src_index.shape[1]
    rel_count = relations.shape[0]
    digits = len(digits_of(count))
    owners = min(MAX_OWNERS, count)
    pay_rows = width * (slots // LANES)
    meta_rows = 2 * (slots // LANES) + rows_count // LANES
    rel_rows = rel_count * (width // LANES)
    vmem, smem = (pl.BlockSpec(memory_space=space) for space in (pltpu.VMEM, pltpu.SMEM))
    dma = pltpu.SemaphoreType.DMA
    pieces = tuple(
        pltpu.VMEM((ROUNDS * 2, size, pay_rows // size, LANES), BF)
        for _, size in digits_of(count)
    )
    arriving = tuple(
        (pltpu.VMEM((size, pay_rows // size, LANES), BF),) * (ROUNDS * 2)
        for _, size in digits_of(count)
    )
    out = pl.pallas_call(
        functools.partial(kernel, count, owners),
        out_shape=(
            jax.ShapeDtypeStruct((rows_count, width), F32),
            jax.ShapeDtypeStruct((rows_count // LANES, LANES), F32),
            jax.ShapeDtypeStruct((rel_count, width), F32),
            jax.ShapeDtypeStruct((rel_count, width), F32),
        ),
        in_specs=[smem, smem] + [pl.BlockSpec(memory_space=pltpu.HBM)] * 8,
        out_specs=(vmem,) * 4,
        scratch_shapes=[
            pltpu.VMEM((rows_count, width), F32),
            pltpu.VMEM((rows_count // LANES, LANES), F32),
            pltpu.VMEM((rel_count, width), F32),
            pltpu.VMEM((rel_count, width), F32),
            pltpu.VMEM(src_index.shape, jnp.int32),
            pltpu.VMEM(dst_index.shape, jnp.int32),
            pltpu.VMEM(rel_index.shape, jnp.int32),
            pltpu.VMEM(neg_index.shape, jnp.int32),
            (pltpu.VMEM((count, meta_rows, LANES), jnp.int32),) * ROUNDS,
            pltpu.VMEM((ROUNDS, 2, pay_rows, LANES), BF),
            arriving,
            pieces,
            pltpu.VMEM((ROUNDS, 2, digits, pay_rows, LANES), BF),
            pltpu.VMEM((rows_count, width), F32),
            pltpu.VMEM((ROUNDS, width, rows_count), BF),
            pltpu.VMEM((ROUNDS, rows_count, slots), BF),
            pltpu.VMEM((ROUNDS, rel_rows, LANES), F32),
            pltpu.VMEM((ROUNDS, count * (rel_rows // owners), LANES), F32),
            pltpu.VMEM((ROUNDS, rel_rows, LANES), F32),
            dma((ROUNDS, 2, digits, 2)),
            dma((ROUNDS, 2, digits, 2)),
            dma((ROUNDS,)),
            dma((ROUNDS,)),
            dma((ROUNDS,)),
            dma((ROUNDS,)),
            dma((ROUNDS,)),
            dma((ROUNDS,)),
            dma((8,)),
        ],
        compiler_params=pltpu.CompilerParams(
            collective_id=0, has_side_effects=True, vmem_limit_bytes=62 * 2**20
        ),
    )(
        matching,
        counts.reshape(ROUNDS),
        embeddings,
        emb_state.reshape(rows_count // LANES, LANES),
        relations,
        rel_state,
        src_index,
        dst_index,
        rel_index,
        neg_index,
    )
    out = pl.pallas_call(
        store,
        out_shape=tuple(jax.ShapeDtypeStruct(x.shape, x.dtype) for x in out),
        in_specs=[vmem] * 4,
        out_specs=(pl.BlockSpec(memory_space=pltpu.HBM),) * 4,
        scratch_shapes=[dma((4,))],
    )(*out)
    return out[0], out[1].reshape(rows_count), out[2], out[3]


def solution(mesh):
    return jax.shard_map(
        functools.partial(on_device, mesh.shape["dom"]),
        mesh=mesh,
        in_specs=(
            P("dom", None),
            P("dom"),
            P(),
            P(),
            P(),
            P(None, "dom"),
            P(None, "dom"),
            P(None, "dom"),
            P(None, "dom"),
            P(None, "dom"),
        ),
        out_specs=(P("dom", None), P("dom"), P(), P()),
        check_vma=False,
    )
```
